768 devices in a mesh: expert: 8 (over y), dp: 96 (over x, z, core).
Axes of the slice: x: 4, y: 8, z: 12, core: 2. Of those that a mesh axis runs over, the one named last changes fastest.
Arguments:
- out_grad: bfloat16 [98304, 2048], P(('expert', 'dp')), may hold values from -6 to 6
- routes: int32 [98304, 6], P(('expert', 'dp')), may hold values from 0 to 63, all different within a row; in each aligned block of 128 rows (0 to 127, 128 to 255, ...) at most 32 rows name the same one
- gates: float32 [98304, 6], P(('expert', 'dp')), may hold values from 0.1 to 1
- saved_hidden: bfloat16 [8, 96, 8, 32, 768], P('expert', 'dp'), may hold values from -20 to 20
- down_weight: bfloat16 [8, 768, 2048], P('expert'), may hold values from -0.125 to 0.125
Outputs:
- d_hidden: bfloat16 [98304, 6, 768], P(('expert', 'dp'))
- weight_grad: float32 [8, 768, 2048], P('expert', 'dp')
The draws below stay inside these ranges and needn't reach their ends.
Inputs may be any that keep to these rules, and one draw needn't show every extreme that they name: `routes`: each token names 6 different experts; among the tokens of one device no expert is named by more than 32 slots, a bound that some block reaches. Entries of saved_hidden at positions that no live slot takes are not read.
All inputs are finite; a program needn't handle non-finite values.
Results may differ from the reference program's by a relative error of at most 0.0049.
Values may be sent and summed in bfloat16 or wider, within the bound.
A program may use at most 64 MiB of HBM per device.

```python
import math
import jax
import jax.numpy as jnp
import numpy as np
from jax import lax

D = 2048
EXPERTS_ALL = 64
TOP = 6
FF_WIN = 768
CAP = 32
TOK_DEV = 128
WIN = 8
TOKENS = 98304
N_EXPERT = 8
N_DP = 96


def spiked(array, rng, source, target, parts, factor):
    def block_of(dim):
        return (jnp.arange(array.shape[dim]) // (array.shape[dim] // parts)).reshape((-1,) + (1,) * (array.ndim - 1 - dim))

    one_side = jax.random.permutation(rng, parts)[block_of(target)]
    second = (block_of(target) + parts // 2) % parts
    return jnp.where((block_of(source) == one_side) | (block_of(source) == second), factor * array, array)


def block_levels(key, dims, shards, low, largest):
    level, own = 1.0, jax.random.fold_in(key, 6)
    for dim, parts in shards:
        steps = jnp.exp(jax.random.uniform(jax.random.fold_in(own, dim), (parts,), jnp.float32, low / len(shards), largest / len(shards)))
        level = level * jnp.repeat(steps, dims[dim] // parts).reshape([-1 if axis == dim else 1 for axis in range(len(dims))])
    return level


def assign_block(key, own, number, rows, count, top, bound, slope):
    order = jax.random.permutation(key, count)
    crowded, common = load_shares(count, rows * top, bound, slope, True), load_shares(count, rows * top, bound, slope, False)
    places = jnp.arange(count)

    def named(sizes, turn):
        used = int((sizes > 0).sum())
        fixed = max(1, used // 4)
        shifted = fixed + (places - fixed + turn * (used - fixed)) % max(1, count - fixed)
        return jnp.zeros((count,), jnp.int32).at[order[jnp.where(places < fixed, places, shifted)]].set(jnp.asarray(sizes, jnp.int32))

    sizes = jnp.where(number % 4 == 0, named(crowded, number // 4), named(common, number - number // 4 - 1))
    mixed = jax.random.permutation(jax.random.fold_in(own, 3), count)
    giver, sink = mixed[0:count // 2 * 2:2], mixed[1:count // 2 * 2:2]
    room = jnp.minimum(sizes[giver] - 1, bound - sizes[sink]) // 2
    room = jnp.where((giver == order[0]) | (sink == order[0]) | (sizes[sink] == 0), 0, jnp.maximum(room, 0))
    shifted = jax.random.randint(jax.random.fold_in(own, 4), (count // 2,), 0, 1 << 20) % (room + 1)
    sizes = sizes.at[giver].add(-shifted).at[sink].add(shifted)
    labels = jnp.searchsorted(jnp.cumsum(sizes), jnp.arange(rows * top), side="right").astype(jnp.int32)
    table = labels.reshape(top, rows).T
    table = table[jax.random.permutation(jax.random.fold_in(own, 1), rows)]
    turn = jax.random.randint(jax.random.fold_in(own, 2), (rows, 1), 0, top)
    return jnp.take_along_axis(table, (jnp.arange(top)[None, :] + turn) % top, axis=1)


def load_shares(number_of, total, bound, slope, full):
    weights = [(1 << 20) // math.isqrt(rank ** slope) + 1 for rank in range(1, number_of + 1)]
    largest = bound if full else min(bound, max(-(-total // number_of), total * weights[0] // sum(weights)))
    least = 1 if total - largest >= number_of - 1 else 0
    given, spare = [largest] + [least] * (number_of - 1), total - largest - least * (number_of - 1)
    while spare > 0:
        free = [i for i in range(1, number_of) if given[i] < largest] or [i for i in range(1, number_of) if given[i] < bound]
        whole, budget = sum([weights[i] for i in free]), spare
        for i in free:
            extra = min(bound - given[i], max(1, budget * weights[i] // whole), spare)
            given[i] = given[i] + extra
            spare = spare - extra
    return np.array(given)


def centred(stream_key, extent, scale, bound, split=(), kind=jnp.bfloat16):
    array = scale * jax.random.normal(stream_key, extent, jnp.float32)
    if split:
        array = array * block_levels(stream_key, extent, split, -0.22, 0.18)
    return jnp.clip(array, -bound, bound).astype(kind)


def heavy_noise(key, extent, width, limit, pieces, heavy, kind=jnp.bfloat16):
    array = width * jax.random.normal(key, extent, jnp.float32)
    if pieces:
        array = array * block_levels(key, extent, pieces, -0.22, 0.18)
    return jnp.clip(spiked(array, jax.random.fold_in(key, 3), *heavy), -limit, limit).astype(kind)


def setup_inputs(seed: int = 0) -> dict:
    streams_of = jax.random.split(jax.random.key(seed), 6)
    out_grad = centred(streams_of[0], (TOKENS, D), 1.0, 6.0, ((0, 768),))
    routes_keys = jax.random.split(jax.random.fold_in(streams_of[1], 1), TOKENS // TOK_DEV)
    routes_turns = jax.random.permutation(jax.random.fold_in(streams_of[1], 3), TOKENS // TOK_DEV)
    routes = jax.vmap(lambda own, number: assign_block(jax.random.fold_in(streams_of[1], 2), own, number, TOK_DEV, EXPERTS_ALL, TOP, CAP, 2))(routes_keys, routes_turns).reshape((TOKENS, TOP))
    gates = jnp.clip(jnp.exp(math.log(1.0) - 2.3025851 * jax.random.uniform(streams_of[2], (TOKENS, TOP), jnp.float32) ** block_levels(streams_of[2], (TOKENS, TOP), ((0, 768),), -0.2, 0.2)), 0.1, 1.0)
    saved_hidden = heavy_noise(streams_of[3], (N_EXPERT, N_DP, N_EXPERT, CAP, FF_WIN), 1.0, 20.0, ((0, 8), (1, 96)), (1, 4, 96, 4.75))
    down_weight = centred(streams_of[4], (WIN, FF_WIN, D), D ** -0.5, 0.125, ((0, 8),))
    return dict(out_grad=out_grad, routes=routes, gates=gates, saved_hidden=saved_hidden, down_weight=down_weight)


def reference(out_grad, routes, gates, saved_hidden, down_weight):
    slot_count = TOK_DEV * TOP
    grad_scale = 1.0 / math.sqrt(TOKENS * TOP / EXPERTS_ALL)
    grads_blocks = out_grad.reshape(N_EXPERT, N_DP, TOK_DEV, D)
    route_blocks = routes.reshape(N_EXPERT, N_DP, slot_count)
    gate_blocks = gates.reshape(N_EXPERT, N_DP, TOK_DEV, TOP)
    weight_wide = down_weight.astype(jnp.float32)
    experts_iota = jnp.arange(N_EXPERT, dtype=jnp.int32)

    def place_rows(target_row, values):
        buffer = jnp.zeros((N_EXPERT * CAP + 1, D), jnp.bfloat16)
        return buffer.at[target_row].set(values)[:N_EXPERT * CAP]

    def one_group(total, group_index):
        grad_group = lax.dynamic_index_in_dim(grads_blocks, group_index, 1, keepdims=False)
        route_group = lax.dynamic_index_in_dim(route_blocks, group_index, 1, keepdims=False)
        gate_group = lax.dynamic_index_in_dim(gate_blocks, group_index, 1, keepdims=False)
        hidden_group = lax.dynamic_index_in_dim(saved_hidden, group_index, 1, keepdims=False)
        inside = route_group < N_EXPERT
        onehot = (route_group[:, :, None] == experts_iota[None, None, :]).astype(jnp.int32)
        position = lax.optimization_barrier(jnp.sum((jnp.cumsum(onehot, axis=1) - onehot) * onehot, axis=2))
        target = jnp.where(inside, route_group * CAP + position, N_EXPERT * CAP).astype(jnp.int32)
        scaled = (gate_group[:, :, :, None] * grad_group[:, :, None, :].astype(jnp.float32)).astype(jnp.bfloat16)
        scaled = scaled.reshape(N_EXPERT, slot_count, D)
        buffers = jax.vmap(place_rows)(target, scaled).reshape(N_EXPERT, N_EXPERT, CAP, D)
        rows_wide = buffers.astype(jnp.float32)
        hidden_grad = jnp.einsum('secd,efd->secf', rows_wide, weight_wide, precision=lax.Precision.HIGHEST).astype(jnp.bfloat16)
        flat_grads = hidden_grad.reshape(N_EXPERT, N_EXPERT * CAP, FF_WIN)
        clamped = jnp.minimum(target, N_EXPERT * CAP - 1).astype(jnp.int32)
        picked = jnp.take_along_axis(flat_grads, clamped[:, :, None], axis=1)
        slot_grads = jnp.where(inside[:, :, None], picked, jnp.zeros_like(picked))
        wgrad_term = jnp.einsum('escf,secd->efd', hidden_group.astype(jnp.float32), rows_wide, precision=lax.Precision.HIGHEST)
        return (total + wgrad_term, slot_grads)
    start_total = jnp.zeros((N_EXPERT, FF_WIN, D), jnp.float32)
    total, slot_grads = lax.scan(one_group, start_total, jnp.arange(N_DP, dtype=jnp.int32))
    d_hidden = jnp.moveaxis(slot_grads, 0, 1).reshape(TOKENS, TOP, FF_WIN)
    weight_grad = total * grad_scale
    return (d_hidden, weight_grad)
```

```python
import functools
import math

import jax
import jax.numpy as jnp
from jax import lax
from jax.experimental import pallas as pl
from jax.experimental.pallas import tpu as pltpu
from jax.sharding import PartitionSpec as P

EXPERTS_ALL = 64
MESH = pl.DeviceIdType.MESH
NY, NX, NZ, NC = 8, 4, 12, 2
CAP = 32
TOK = 128
TOP = 6
D = 2048
FF = 768
NCH = 8
CW = D // NCH
HW = CW // 2
Y_ORDER = (4, 3, 5, 2, 6, 1, 7)
X_ORDER = (2, 1, 3)
Z_ORDER = (6, 5, 7, 4, 8, 3, 9, 2, 10, 1, 11)
F32, BF16 = jnp.float32, jnp.bfloat16


def kernel(
    scale,
    og_hbm, rt_ref, gt_ref, hid_hbm, w_hbm,
    dh_hbm, wg_hbm,
    og, hid, hid_t, wv, outb, recv, acc, back, got, pick, dh,
    wg, cr, xf, xs, xr, zf, zs, zr, wgo,
    in_sem, w_sem, out_sem,
    ys_sem, yr_sem, bs_sem, br_sem, cs_sem, cr_sem, xs_sem, xr_sem, zs_sem, zr_sem,
):
    y = lax.axis_index("expert")
    dp = lax.axis_index("dp")
    c = lax.rem(dp, NC)
    z = lax.rem(dp // NC, NZ)
    x = dp // (NC * NZ)

    def dev_y(d):
        return (lax.rem(y + d, NY), dp)

    def dev_c():
        return (y, dp + 1 - 2 * c)

    def dev_x(d):
        return (y, (lax.rem(x + d, NX) * NZ + z) * NC + c)

    def dev_z(d):
        return (y, (x * NZ + lax.rem(z + d, NZ)) * NC + c)

    barrier = pltpu.get_barrier_semaphore()
    peers = [dev_z(d) for d in Z_ORDER] + [dev_y(d) for d in Y_ORDER]
    peers += [dev_x(d) for d in X_ORDER] + [dev_c()]
    for p in peers:
        pl.semaphore_signal(barrier, inc=1, device_id=p, device_id_type=MESH)

    def remote(src, dst, ssem, rsem, dev):
        return pltpu.make_async_remote_copy(
            src_ref=src, dst_ref=dst, send_sem=ssem, recv_sem=rsem,
            device_id=dev, device_id_type=MESH,
        )

    def disp(ch, d):
        return remote(
            outb.at[ch, lax.rem(y + d, NY)], recv.at[ch, y],
            ys_sem.at[ch, d - 1], yr_sem.at[ch, d - 1], dev_y(d),
        )

    def ret(d):
        return remote(
            back.at[lax.rem(y + d, NY)], got.at[y], bs_sem.at[d - 1], br_sem.at[d - 1], dev_y(d)
        )

    def core(ch):
        return remote(wg.at[ch, :, 1 - c], cr.at[ch], cs_sem.at[ch], cr_sem.at[ch], dev_c())

    def xcopy(ch, d):
        return remote(
            xs.at[ch, lax.rem(x + d, NX)], xr.at[ch, d - 1],
            xs_sem.at[ch, d - 1], xr_sem.at[ch, d - 1], dev_x(d),
        )

    def zcopy(ch, d):
        return remote(
            zs.at[ch, lax.rem(z + d, NZ)], zr.at[ch, d - 1],
            zs_sem.at[ch, d - 1], zr_sem.at[ch, d - 1], dev_z(d),
        )

    cp_og = pltpu.make_async_copy(og_hbm, og, in_sem.at[0])
    cp_og.start()
    cp_hid = pltpu.make_async_copy(hid_hbm, hid, in_sem.at[1])
    cp_hid.start()
    cp_w = []
    for ch in range(NCH):
        cp = pltpu.make_async_copy(w_hbm.at[:, pl.ds(ch * CW, CW)], wv.at[ch], w_sem.at[ch])
        cp.start()
        cp_w.append(cp)

    routes = rt_ref[...]
    gates = gt_ref[...]
    eid = lax.broadcasted_iota(jnp.int32, (NY, TOK), 0)
    mask = jnp.zeros((NY, TOK), F32)
    gate_e = jnp.zeros((NY, TOK), F32)
    for k in range(TOP):
        hit = routes[k : k + 1, :] == eid
        mask = mask + jnp.where(hit, 1.0, 0.0)
        gate_e = gate_e + jnp.where(hit, gates[k : k + 1, :], 0.0)
    t_row = lax.broadcasted_iota(jnp.int32, (TOK, TOK), 0)
    t_col = lax.broadcasted_iota(jnp.int32, (TOK, TOK), 1)
    before = jnp.where(t_row < t_col, 1.0, 0.0).astype(BF16)
    pos = jnp.dot(mask.astype(BF16), before, preferred_element_type=F32)
    slot = jnp.where(mask > 0.0, pos, -1.0).astype(jnp.int32)
    cid = lax.broadcasted_iota(jnp.int32, (NY, CAP, TOK), 1)
    sel = jnp.where(slot[:, None, :] == cid, 1.0, 0.0)
    gate_row = jnp.sum(sel * gate_e[:, None, :], axis=-1, keepdims=True).reshape(NY * CAP, 1)
    sel = sel.reshape(NY * CAP, TOK).astype(BF16)

    cp_og.wait()
    for ch in range(NCH):
        rows = jnp.dot(sel, og[:, ch * CW : (ch + 1) * CW], preferred_element_type=F32)
        outb[ch] = (rows * gate_row).astype(BF16).reshape(NY, CAP, CW)
        if ch == 0:
            pl.semaphore_wait(barrier, len(peers))
        for d in Y_ORDER:
            disp(ch, d).start()

    for ch in range(NCH):
        recv[ch, y] = outb[ch, y]
    rid = lax.broadcasted_iota(jnp.int32, (NY * CAP, TOK), 0)
    for k in range(TOP):
        hit = routes[k : k + 1, :] == eid
        pos_k = jnp.sum(jnp.where(hit, pos, 0.0), axis=0, keepdims=True).astype(jnp.int32)
        r_k = routes[k : k + 1, :]
        target = jnp.where(r_k < NY, r_k * CAP + pos_k, -1)
        pick[k] = jnp.where(rid == target, 1.0, 0.0).T.astype(BF16)
    cp_hid.wait()
    hid_t[...] = hid[...].T

    def stage_core(ch):
        core(ch).wait_recv()
        s = wg[ch, :, c] + cr[ch]
        s = jnp.concatenate([s[:, :, :HW], s[:, :, HW:]], axis=1)
        s = s.reshape(NX, NZ, 16, HW)
        xf[ch] = s
        xs[ch] = s.astype(BF16)
        for d in X_ORDER:
            xcopy(ch, d).start()

    def stage_x(ch):
        for d in X_ORDER:
            xcopy(ch, d).wait_recv()
        s = xf[ch, x]
        for d in X_ORDER:
            s = s + xr[ch, d - 1].astype(F32)
        zf[ch] = s
        zs[ch] = s.astype(BF16)
        for d in Z_ORDER:
            zcopy(ch, d).start()

    def stage_z(ch):
        for d in Z_ORDER:
            zcopy(ch, d).wait_recv()
        s = zf[ch, z]
        for d in Z_ORDER:
            s = s + zr[ch, d - 1].astype(F32)
        s = s * scale
        wgo[:, ch * CW : ch * CW + HW] = s[:8]
        wgo[:, ch * CW + HW : (ch + 1) * CW] = s[8:]

    for ch in range(NCH):
        for d in Y_ORDER:
            disp(ch, d).wait_recv()
        cp_w[ch].wait()
        rows = recv[ch].reshape(NY * CAP, CW)
        part = lax.dot_general(
            rows, wv[ch], (((1,), (1,)), ((), ())), preferred_element_type=F32
        )
        if ch == 0:
            acc[...] = part
        elif ch < NCH - 1:
            acc[...] += part
        else:
            back[...] = (acc[...] + part).astype(BF16).reshape(NY, CAP, FF)
            for d in Y_ORDER:
                ret(d).start()
        term = jnp.dot(hid_t[...], rows, preferred_element_type=F32)
        wg[ch] = term.reshape(NX * NZ, NC, 8, CW)
        core(ch).start()
        if ch >= 1:
            stage_core(ch - 1)
        if ch >= 2:
            stage_x(ch - 2)
        if ch >= 4:
            stage_z(ch - 4)
    got[y] = back[y]
    stage_core(NCH - 1)
    stage_x(NCH - 2)
    stage_x(NCH - 1)
    for ch in range(NCH - 4, NCH - 1):
        stage_z(ch)

    for d in Y_ORDER:
        ret(d).wait_recv()
    rows = got[...].reshape(NY * CAP, FF)
    outs = []
    for k in range(TOP):
        dh[k] = jnp.dot(pick[k], rows, preferred_element_type=F32).astype(BF16)
        cp = pltpu.make_async_copy(dh.at[k], dh_hbm.at[k], out_sem.at[k])
        cp.start()
        outs.append(cp)
    stage_z(NCH - 1)
    cp = pltpu.make_async_copy(wgo, wg_hbm, out_sem.at[TOP])
    cp.start()
    outs.append(cp)

    for ch in range(NCH):
        for d in Y_ORDER:
            disp(ch, d).wait_send()
        core(ch).wait_send()
        for d in X_ORDER:
            xcopy(ch, d).wait_send()
        for d in Z_ORDER:
            zcopy(ch, d).wait_send()
    for d in Y_ORDER:
        ret(d).wait_send()
    for cp in outs:
        cp.wait()


def on_device(out_grad, routes, gates, saved_hidden, down_weight):
    scale = 1.0 / math.sqrt(TOK * NY * NX * NZ * NC * TOP / EXPERTS_ALL)
    any_ = pl.BlockSpec(memory_space=pl.ANY)
    vmem = pl.BlockSpec(memory_space=pltpu.VMEM)
    dma = pltpu.SemaphoreType.DMA
    dh, wg = pl.pallas_call(
        functools.partial(kernel, scale),
        out_shape=(
            jax.ShapeDtypeStruct((TOP, TOK, FF), BF16),
            jax.ShapeDtypeStruct((8, D), F32),
        ),
        in_specs=[any_, vmem, vmem, any_, any_],
        out_specs=(any_, any_),
        scratch_shapes=[
            pltpu.VMEM((TOK, D), BF16),
            pltpu.VMEM((NY * CAP, FF), BF16),
            pltpu.VMEM((FF, NY * CAP), BF16),
            pltpu.VMEM((NCH, FF, CW), BF16),
            pltpu.VMEM((NCH, NY, CAP, CW), BF16),
            pltpu.VMEM((NCH, NY, CAP, CW), BF16),
            pltpu.VMEM((NY * CAP, FF), F32),
            pltpu.VMEM((NY, CAP, FF), BF16),
            pltpu.VMEM((NY, CAP, FF), BF16),
            pltpu.VMEM((TOP, TOK, NY * CAP), BF16),
            pltpu.VMEM((TOP, TOK, FF), BF16),
            pltpu.VMEM((NCH, NX * NZ, NC, 8, CW), F32),
            pltpu.VMEM((NCH, NX * NZ, 8, CW), F32),
            pltpu.VMEM((NCH, NX, NZ, 16, HW), F32),
            pltpu.VMEM((NCH, NX, NZ, 16, HW), BF16),
            pltpu.VMEM((NCH, NX - 1, NZ, 16, HW), BF16),
            pltpu.VMEM((NCH, NZ, 16, HW), F32),
            pltpu.VMEM((NCH, NZ, 16, HW), BF16),
            pltpu.VMEM((NCH, NZ - 1, 16, HW), BF16),
            pltpu.VMEM((8, D), F32),
            dma((2,)),
            dma((NCH,)),
            dma((TOP + 1,)),
            dma((NCH, NY - 1)),
            dma((NCH, NY - 1)),
            dma((NY - 1,)),
            dma((NY - 1,)),
            dma((NCH,)),
            dma((NCH,)),
            dma((NCH, NX - 1)),
            dma((NCH, NX - 1)),
            dma((NCH, NZ - 1)),
            dma((NCH, NZ - 1)),
        ],
        compiler_params=pltpu.CompilerParams(
            collective_id=0, has_side_effects=True, vmem_limit_bytes=48 << 20
        ),
        name="moe_down_bwd",
    )(
        out_grad,
        routes.T,
        gates.T,
        saved_hidden.reshape(NY * CAP, FF),
        down_weight[0],
    )
    return dh.transpose(1, 0, 2), wg[None]


def solution(mesh):
    return jax.shard_map(
        on_device,
        mesh=mesh,
        in_specs=(
            P(("expert", "dp"), None),
            P(("expert", "dp"), None),
            P(("expert", "dp"), None),
            P("expert", "dp", None, None, None),
            P("expert", None, None),
        ),
        out_specs=(P(("expert", "dp"), None, None), P("expert", "dp", None)),
        check_vma=False,
    )
```

```python
import functools
import math

import jax
import jax.numpy as jnp
from jax import lax
from jax.experimental import pallas as pl
from jax.experimental.pallas import tpu as pltpu
from jax.sharding import PartitionSpec as P

EXPERTS_ALL = 64
MESH = pl.DeviceIdType.MESH
NY, NX, NZ, NC = 8, 4, 12, 2
CAP = 32
TOK = 128
TOP = 6
D = 2048
FF = 768
WIDTHS = (256,) * 8
ZGROUPS = ((0, 1), (2, 3), (4, 5), (6,), (7,))
NCH = len(WIDTHS)
OFFS = tuple(sum(WIDTHS[:i]) for i in range(NCH))
NZG = len(ZGROUPS)
ZROWS = tuple(sum(WIDTHS[ch] // 16 for ch in g) for g in ZGROUPS)
VLIM = 62 << 20
Y_ORDER = (4, 3, 5, 2, 6, 1, 7)
X_ORDER = (2, 1, 3)
Z_ORDER = (6, 5, 7, 4, 8, 3, 9, 2, 10, 1, 11)
F32, BF16 = jnp.float32, jnp.bfloat16


def kernel(
    scale,
    og_hbm, rt_hbm, gt_hbm, hid_hbm, w_hbm,
    dh_hbm, wg_hbm,
    rt_ref, gt_ref, og, hid, hid_t, wv, outb, recv, acc, back, got, pick, dh,
    wg, cr, xf, xs, xr, zf, zs, zr, wgo,
    late_sem, in_sem, w_sem, out_sem,
    ys_sem, yr_sem, bs_sem, br_sem, cs_sem, cr_sem, xs_sem, xr_sem, zs_sem, zr_sem,
):
    y = lax.axis_index("expert")
    dp = lax.axis_index("dp")
    c = lax.rem(dp, NC)
    z = lax.rem(dp // NC, NZ)
    x = dp // (NC * NZ)

    def dev_y(d):
        return (lax.rem(y + d, NY), dp)

    def dev_c():
        return (y, dp + 1 - 2 * c)

    def dev_x(d):
        return (y, (lax.rem(x + d, NX) * NZ + z) * NC + c)

    def dev_z(d):
        return (y, (x * NZ + lax.rem(z + d, NZ)) * NC + c)

    def remote(src, dst, ssem, rsem, dev):
        return pltpu.make_async_remote_copy(
            src_ref=src, dst_ref=dst, send_sem=ssem, recv_sem=rsem,
            device_id=dev, device_id_type=MESH,
        )

    def disp(ch, d):
        return remote(
            outb[ch].at[lax.rem(y + d, NY)], recv[ch].at[y],
            ys_sem.at[ch, d - 1], yr_sem.at[ch, d - 1], dev_y(d),
        )

    def ret(d):
        return remote(
            back.at[lax.rem(y + d, NY)], got.at[y], bs_sem.at[d - 1], br_sem.at[d - 1], dev_y(d)
        )

    def core(ch):
        return remote(wg[ch].at[:, 1 - c], cr[ch], cs_sem.at[ch], cr_sem.at[ch], dev_c())

    def xcopy(ch, d):
        return remote(
            xs[ch].at[lax.rem(x + d, NX)], xr[ch].at[d - 1],
            xs_sem.at[ch, d - 1], xr_sem.at[ch, d - 1], dev_x(d),
        )

    def zcopy(g, d):
        return remote(
            zs[g].at[lax.rem(z + d, NZ)], zr[g].at[d - 1],
            zs_sem.at[g, d - 1], zr_sem.at[g, d - 1], dev_z(d),
        )

    cp_rt = pltpu.make_async_copy(rt_hbm, rt_ref, in_sem.at[2])
    cp_rt.start()
    cp_gt = pltpu.make_async_copy(gt_hbm, gt_ref, in_sem.at[3])
    cp_gt.start()
    cp_og = pltpu.make_async_copy(og_hbm, og, in_sem.at[0])
    cp_og.start()
    barrier = pltpu.get_barrier_semaphore()
    peers = [dev_y(d) for d in Y_ORDER] + [dev_x(d) for d in X_ORDER] + [dev_c()]
    for p in peers:
        pl.semaphore_signal(barrier, inc=1, device_id=p, device_id_type=MESH)
    for d in range(1, NZ):

        @pl.when(z + d < NZ)
        def _(d=d):
            pl.semaphore_signal(barrier, inc=1, device_id=dev_z(d), device_id_type=MESH)

    cp_hid = pltpu.make_async_copy(hid_hbm, hid, in_sem.at[1])
    cp_hid.start()
    cp_w = []
    for ch in range(NCH):
        cp = pltpu.make_async_copy(w_hbm.at[:, pl.ds(OFFS[ch], WIDTHS[ch])], wv[ch], w_sem.at[ch])
        cp.start()
        cp_w.append(cp)

    cp_rt.wait()
    cp_gt.wait()
    routes = rt_ref[...]
    gates = gt_ref[...]
    eid = lax.broadcasted_iota(jnp.int32, (NY, TOK), 0)
    mask = jnp.zeros((NY, TOK), F32)
    gate_e = jnp.zeros((NY, TOK), F32)
    for k in range(TOP):
        hit = routes[k : k + 1, :] == eid
        mask = mask + jnp.where(hit, 1.0, 0.0)
        gate_e = gate_e + jnp.where(hit, gates[k : k + 1, :], 0.0)
    t_row = lax.broadcasted_iota(jnp.int32, (TOK, TOK), 0)
    t_col = lax.broadcasted_iota(jnp.int32, (TOK, TOK), 1)
    before = jnp.where(t_row < t_col, 1.0, 0.0).astype(BF16)
    pos = jnp.dot(mask.astype(BF16), before, preferred_element_type=F32)
    slot = jnp.where(mask > 0.0, pos, -1.0).astype(jnp.int32)
    cid = lax.broadcasted_iota(jnp.int32, (NY, CAP, TOK), 1)
    sel = jnp.where(slot[:, None, :] == cid, 1.0, 0.0)
    gate_row = jnp.sum(sel * gate_e[:, None, :], axis=-1, keepdims=True).reshape(NY * CAP, 1)
    sel = sel.reshape(NY * CAP, TOK).astype(BF16)

    cp_og.wait()
    for ch in range(NCH):
        w = WIDTHS[ch]
        rows = jnp.dot(sel, og[:, OFFS[ch] : OFFS[ch] + w], preferred_element_type=F32)
        outb[ch][...] = (rows * gate_row).astype(BF16).reshape(NY, CAP, w)
        if ch == 0:
            pl.semaphore_wait(barrier, len(peers) + z)
        for d in Y_ORDER:
            disp(ch, d).start()

    for d in range(1, NZ):

        @pl.when(z >= d)
        def _(d=d):
            pl.semaphore_signal(late_sem, inc=1, device_id=dev_z(NZ - d), device_id_type=MESH)

    for ch in range(NCH):
        recv[ch][y] = outb[ch][y]
    rid = lax.broadcasted_iota(jnp.int32, (NY * CAP, TOK), 0)
    for k in range(TOP):
        hit = routes[k : k + 1, :] == eid
        pos_k = jnp.sum(jnp.where(hit, pos, 0.0), axis=0, keepdims=True).astype(jnp.int32)
        r_k = routes[k : k + 1, :]
        target = jnp.where(r_k < NY, r_k * CAP + pos_k, -1)
        pick[k] = jnp.where(rid == target, 1.0, 0.0).T.astype(BF16)
    cp_hid.wait()
    hid_t[...] = hid[...].T

    def stage_core(ch):
        w = WIDTHS[ch]
        core(ch).wait_recv()
        s = wg[ch][:, c] + cr[ch][...]
        s = jnp.concatenate([s[:, :, i : i + 128] for i in range(0, w, 128)], axis=1)
        xf[ch][...] = s.reshape(NX, NZ, w // 16, 128)
        xs[ch][...] = s.reshape(NX, NZ * w // 16, 128).astype(BF16)
        for d in X_ORDER:
            xcopy(ch, d).start()

    def stage_x(ch):
        w = WIDTHS[ch]
        for d in X_ORDER:
            xcopy(ch, d).wait_recv()
        s = xf[ch][x].reshape(NZ * w // 16, 128)
        for d in X_ORDER:
            s = s + xr[ch][d - 1].astype(F32)
        s = s.reshape(NZ, w // 16, 128)
        g = next(i for i in range(NZG) if ch in ZGROUPS[i])
        o = sum(WIDTHS[i] // 16 for i in ZGROUPS[g] if i < ch)
        zf[g][:, o : o + w // 16] = s
        if ch == ZGROUPS[g][-1]:
            zs[g][...] = zf[g][...].astype(BF16)
            if g == 0:

                @pl.when(z < NZ - 1)
                def _():
                    pl.semaphore_wait(late_sem, NZ - 1 - z)

            for d in Z_ORDER:
                zcopy(g, d).start()

    def stage_z(g):
        for d in Z_ORDER:
            zcopy(g, d).wait_recv()
        s = zf[g][z]
        for d in Z_ORDER:
            s = s + zr[g][d - 1].astype(F32)
        s = s * scale
        r = 0
        for ch in ZGROUPS[g]:
            for o in range(OFFS[ch], OFFS[ch] + WIDTHS[ch], 128):
                wgo[:, o : o + 128] = s[r : r + 8]
                r += 8

    def stage_d(ch):
        for d in Y_ORDER:
            disp(ch, d).wait_recv()
        rows = recv[ch][...].reshape(NY * CAP, WIDTHS[ch])
        term = jnp.dot(hid_t[...], rows, preferred_element_type=F32)
        wg[ch][...] = term.reshape(NX * NZ, NC, 8, WIDTHS[ch])
        core(ch).start()

    def stage_h(ch):
        cp_w[ch].wait()
        part = lax.dot_general(
            recv[ch][...].reshape(NY * CAP, WIDTHS[ch]), wv[ch][...],
            (((1,), (1,)), ((), ())), preferred_element_type=F32,
        )
        if ch == 0:
            acc[...] = part
        elif ch < NCH - 1:
            acc[...] += part
        else:
            back[...] = (acc[...] + part).astype(BF16).reshape(NY, CAP, FF)
            for d in Y_ORDER:
                ret(d).start()

    for ch in range(NCH):
        stage_d(ch)
        stage_h(ch)
        if ch >= 2:
            stage_x(ch - 2)
        stage_core(ch)
    stage_x(NCH - 2)
    stage_x(NCH - 1)
    got[y] = back[y]

    for d in Y_ORDER:
        ret(d).wait_recv()
    rows = got[...].reshape(NY * CAP, FF)
    outs = []
    for k in range(TOP):
        dh[k] = jnp.dot(pick[k], rows, preferred_element_type=F32).astype(BF16)
        cp = pltpu.make_async_copy(dh.at[k], dh_hbm.at[k], out_sem.at[k])
        cp.start()
        outs.append(cp)
    for ch in range(NCH):
        for d in Y_ORDER:
            disp(ch, d).wait_send()
        core(ch).wait_send()
        for d in X_ORDER:
            xcopy(ch, d).wait_send()
    for d in Y_ORDER:
        ret(d).wait_send()
    for g in range(NZG):
        for d in Z_ORDER:
            zcopy(g, d).wait_send()
    for g in range(NZG):
        stage_z(g)
    cp = pltpu.make_async_copy(wgo, wg_hbm, out_sem.at[TOP])
    cp.start()
    outs.append(cp)
    for cp in outs:
        cp.wait()


def on_device(out_grad, routes, gates, saved_hidden, down_weight):
    scale = 1.0 / math.sqrt(TOK * NY * NX * NZ * NC * TOP / EXPERTS_ALL)
    any_ = pl.BlockSpec(memory_space=pl.ANY)
    hbm = pl.BlockSpec(memory_space=pltpu.HBM)
    dma = pltpu.SemaphoreType.DMA
    dh, wg = pl.pallas_call(
        functools.partial(kernel, scale),
        out_shape=(
            jax.ShapeDtypeStruct((TOP, TOK, FF), BF16),
            jax.ShapeDtypeStruct((8, D), F32),
        ),
        in_specs=[hbm] * 5,
        out_specs=(any_, any_),
        scratch_shapes=[
            pltpu.VMEM((TOP, TOK), jnp.int32),
            pltpu.VMEM((TOP, TOK), F32),
            pltpu.VMEM((TOK, D), BF16),
            pltpu.VMEM((NY * CAP, FF), BF16),
            pltpu.VMEM((FF, NY * CAP), BF16),
            [pltpu.VMEM((FF, w), BF16) for w in WIDTHS],
            [pltpu.VMEM((NY, CAP, w), BF16) for w in WIDTHS],
            [pltpu.VMEM((NY, CAP, w), BF16) for w in WIDTHS],
            pltpu.VMEM((NY * CAP, FF), F32),
            pltpu.VMEM((NY, CAP, FF), BF16),
            pltpu.VMEM((NY, CAP, FF), BF16),
            pltpu.VMEM((TOP, TOK, NY * CAP), BF16),
            pltpu.VMEM((TOP, TOK, FF), BF16),
            [pltpu.VMEM((NX * NZ, NC, 8, w), F32) for w in WIDTHS],
            [pltpu.VMEM((NX * NZ, 8, w), F32) for w in WIDTHS],
            [pltpu.VMEM((NX, NZ, w // 16, 128), F32) for w in WIDTHS],
            [pltpu.VMEM((NX, NZ * w // 16, 128), BF16) for w in WIDTHS],
            [pltpu.VMEM((NX - 1, NZ * w // 16, 128), BF16) for w in WIDTHS],
            [pltpu.VMEM((NZ, r, 128), F32) for r in ZROWS],
            [pltpu.VMEM((NZ, r, 128), BF16) for r in ZROWS],
            [pltpu.VMEM((NZ - 1, r, 128), BF16) for r in ZROWS],
            pltpu.VMEM((8, D), F32),
            pltpu.SemaphoreType.REGULAR,
            dma((4,)),
            dma((NCH,)),
            dma((TOP + 1,)),
            dma((NCH, NY - 1)),
            dma((NCH, NY - 1)),
            dma((NY - 1,)),
            dma((NY - 1,)),
            dma((NCH,)),
            dma((NCH,)),
            dma((NCH, NX - 1)),
            dma((NCH, NX - 1)),
            dma((NZG, NZ - 1)),
            dma((NZG, NZ - 1)),
        ],
        compiler_params=pltpu.CompilerParams(
            collective_id=0, has_side_effects=True, vmem_limit_bytes=VLIM
        ),
        name="moe_down_bwd",
    )(
        out_grad,
        routes.T,
        gates.T,
        saved_hidden.reshape(NY * CAP, FF),
        down_weight[0],
    )
    return dh.transpose(1, 0, 2), wg[None]


def solution(mesh):
    return jax.shard_map(
        on_device,
        mesh=mesh,
        in_specs=(
            P(("expert", "dp"), None),
            P(("expert", "dp"), None),
            P(("expert", "dp"), None),
            P("expert", "dp", None, None, None),
            P("expert", None, None),
        ),
        out_specs=(P(("expert", "dp"), None, None), P("expert", "dp", None)),
        check_vma=False,
    )
```

```python
import functools
import math

import jax
import jax.numpy as jnp
from jax import lax
from jax.experimental import pallas as pl
from jax.experimental.pallas import tpu as pltpu
from jax.sharding import PartitionSpec as P

EXPERTS_ALL = 64
MESH = pl.DeviceIdType.MESH
NY, NX, NZ, NC = 8, 4, 12, 2
CAP = 32
TOK = 128
TOP = 6
D = 2048
FF = 768
WIDTHS = (256,) * 8
ZGROUPS = ((0, 1), (2, 3), (4, 5), (6,), (7,))
NCH = len(WIDTHS)
OFFS = tuple(sum(WIDTHS[:i]) for i in range(NCH))
NZG = len(ZGROUPS)
ZROWS = tuple(sum(WIDTHS[ch] // 16 for ch in g) for g in ZGROUPS)
UGRID = 2
VLIM = 62 << 20
Y_ORDER = (4, 3, 5, 2, 6, 1, 7)
X_ORDER = (2, 1, 3)
Z_ORDER = (6, 5, 7, 4, 8, 3, 9, 2, 10, 1, 11)
F32, BF16 = jnp.float32, jnp.bfloat16


def kernel(
    scale,
    og_hbm, rt_hbm, gt_hbm, hid_hbm, w_hbm,
    got_hbm, pick_hbm, wg_hbm,
    rt_ref, gt_ref, og, hid, hid_t, wv, outb, recv, acc, back, got, pick,
    wg, cr, xf, xs, xr, zf, zs, zr, wgo,
    late_sem, in_sem, w_sem, out_sem,
    ys_sem, yr_sem, bs_sem, br_sem, cs_sem, cr_sem, xs_sem, xr_sem, zs_sem, zr_sem,
):
    y = lax.axis_index("expert")
    dp = lax.axis_index("dp")
    c = lax.rem(dp, NC)
    z = lax.rem(dp // NC, NZ)
    x = dp // (NC * NZ)

    def dev_y(d):
        return (lax.rem(y + d, NY), dp)

    def dev_c():
        return (y, dp + 1 - 2 * c)

    def dev_x(d):
        return (y, (lax.rem(x + d, NX) * NZ + z) * NC + c)

    def dev_z(d):
        return (y, (x * NZ + lax.rem(z + d, NZ)) * NC + c)

    def remote(src, dst, ssem, rsem, dev):
        return pltpu.make_async_remote_copy(
            src_ref=src, dst_ref=dst, send_sem=ssem, recv_sem=rsem,
            device_id=dev, device_id_type=MESH,
        )

    def disp(ch, d):
        return remote(
            outb[ch].at[lax.rem(y + d, NY)], recv[ch].at[y],
            ys_sem.at[ch, d - 1], yr_sem.at[ch, d - 1], dev_y(d),
        )

    def ret(d):
        return remote(
            back.at[lax.rem(y + d, NY)], got.at[y], bs_sem.at[d - 1], br_sem.at[d - 1], dev_y(d)
        )

    def core(ch):
        return remote(wg[ch].at[:, 1 - c], cr[ch], cs_sem.at[ch], cr_sem.at[ch], dev_c())

    def xcopy(ch, d):
        return remote(
            xs[ch].at[lax.rem(x + d, NX)], xr[ch].at[d - 1],
            xs_sem.at[ch, d - 1], xr_sem.at[ch, d - 1], dev_x(d),
        )

    def zcopy(g, d):
        return remote(
            zs[g].at[lax.rem(z + d, NZ)], zr[g].at[d - 1],
            zs_sem.at[g, d - 1], zr_sem.at[g, d - 1], dev_z(d),
        )

    cp_rt = pltpu.make_async_copy(rt_hbm, rt_ref, in_sem.at[2])
    cp_rt.start()
    cp_gt = pltpu.make_async_copy(gt_hbm, gt_ref, in_sem.at[3])
    cp_gt.start()
    cp_og = pltpu.make_async_copy(og_hbm, og, in_sem.at[0])
    cp_og.start()
    barrier = pltpu.get_barrier_semaphore()
    peers = [dev_y(d) for d in Y_ORDER] + [dev_x(d) for d in X_ORDER] + [dev_c()]
    for p in peers:
        pl.semaphore_signal(barrier, inc=1, device_id=p, device_id_type=MESH)
    for d in range(1, NZ):

        @pl.when(z + d < NZ)
        def _(d=d):
            pl.semaphore_signal(barrier, inc=1, device_id=dev_z(d), device_id_type=MESH)

    cp_hid = pltpu.make_async_copy(hid_hbm, hid, in_sem.at[1])
    cp_hid.start()
    cp_w = []
    for ch in range(NCH):
        cp = pltpu.make_async_copy(w_hbm.at[:, pl.ds(OFFS[ch], WIDTHS[ch])], wv[ch], w_sem.at[ch])
        cp.start()
        cp_w.append(cp)

    cp_rt.wait()
    cp_gt.wait()
    routes = rt_ref[...]
    gates = gt_ref[...]
    eid = lax.broadcasted_iota(jnp.int32, (NY, TOK), 0)
    mask = jnp.zeros((NY, TOK), F32)
    gate_e = jnp.zeros((NY, TOK), F32)
    for k in range(TOP):
        hit = routes[k : k + 1, :] == eid
        mask = mask + jnp.where(hit, 1.0, 0.0)
        gate_e = gate_e + jnp.where(hit, gates[k : k + 1, :], 0.0)
    t_row = lax.broadcasted_iota(jnp.int32, (TOK, TOK), 0)
    t_col = lax.broadcasted_iota(jnp.int32, (TOK, TOK), 1)
    before = jnp.where(t_row < t_col, 1.0, 0.0).astype(BF16)
    pos = jnp.dot(mask.astype(BF16), before, preferred_element_type=F32)
    slot = jnp.where(mask > 0.0, pos, -1.0).astype(jnp.int32)
    cid = lax.broadcasted_iota(jnp.int32, (NY, CAP, TOK), 1)
    sel = jnp.where(slot[:, None, :] == cid, 1.0, 0.0)
    gate_row = jnp.sum(sel * gate_e[:, None, :], axis=-1, keepdims=True).reshape(NY * CAP, 1)
    sel = sel.reshape(NY * CAP, TOK).astype(BF16)

    cp_og.wait()
    for ch in range(NCH):
        w = WIDTHS[ch]
        rows = jnp.dot(sel, og[:, OFFS[ch] : OFFS[ch] + w], preferred_element_type=F32)
        outb[ch][...] = (rows * gate_row).astype(BF16).reshape(NY, CAP, w)
        if ch == 0:
            pl.semaphore_wait(barrier, len(peers) + z)
            for d in range(1, NZ):

                @pl.when(z >= d)
                def _(d=d):
                    pl.semaphore_signal(late_sem, inc=1, device_id=dev_z(NZ - d), device_id_type=MESH)

        for d in Y_ORDER:
            disp(ch, d).start()

    for ch in range(NCH):
        recv[ch][y] = outb[ch][y]
    rid = lax.broadcasted_iota(jnp.int32, (NY * CAP, TOK), 0)
    for k in range(TOP):
        hit = routes[k : k + 1, :] == eid
        pos_k = jnp.sum(jnp.where(hit, pos, 0.0), axis=0, keepdims=True).astype(jnp.int32)
        r_k = routes[k : k + 1, :]
        target = jnp.where(r_k < NY, r_k * CAP + pos_k, -1)
        pick[k] = jnp.where(rid == target, 1.0, 0.0).T.astype(BF16)
    cp_hid.wait()
    cp_pick = pltpu.make_async_copy(pick, pick_hbm, out_sem.at[0])
    cp_pick.start()
    hid_t[...] = hid[...].T

    def stage_core(ch):
        w = WIDTHS[ch]
        core(ch).wait_recv()
        s = wg[ch][:, c] + cr[ch][...]
        s = jnp.concatenate([s[:, :, i : i + 128] for i in range(0, w, 128)], axis=1)
        xf[ch][...] = s.reshape(NX, NZ, w // 16, 128)
        xs[ch][...] = s.reshape(NX, NZ * w // 16, 128).astype(BF16)
        for d in X_ORDER:
            xcopy(ch, d).start()

    def stage_x(ch):
        w = WIDTHS[ch]
        for d in X_ORDER:
            xcopy(ch, d).wait_recv()
        s = xf[ch][x].reshape(NZ * w // 16, 128)
        for d in X_ORDER:
            s = s + xr[ch][d - 1].astype(F32)
        s = s.reshape(NZ, w // 16, 128)
        g = next(i for i in range(NZG) if ch in ZGROUPS[i])
        o = sum(WIDTHS[i] // 16 for i in ZGROUPS[g] if i < ch)
        zf[g][:, o : o + w // 16] = s
        if ch == ZGROUPS[g][-1]:
            zs[g][...] = zf[g][...].astype(BF16)
            if g == 0:

                @pl.when(z < NZ - 1)
                def _():
                    pl.semaphore_wait(late_sem, NZ - 1 - z)

            for d in Z_ORDER:
                zcopy(g, d).start()

    def stage_z(g):
        for d in Z_ORDER:
            zcopy(g, d).wait_recv()
        s = zf[g][z]
        for d in Z_ORDER:
            s = s + zr[g][d - 1].astype(F32)
        s = s * scale
        r = 0
        for ch in ZGROUPS[g]:
            for o in range(OFFS[ch], OFFS[ch] + WIDTHS[ch], 128):
                wgo[:, o : o + 128] = s[r : r + 8]
                r += 8

    def stage_d(ch):
        for d in Y_ORDER:
            disp(ch, d).wait_recv()
        rows = recv[ch][...].reshape(NY * CAP, WIDTHS[ch])
        term = jnp.dot(hid_t[...], rows, preferred_element_type=F32)
        wg[ch][...] = term.reshape(NX * NZ, NC, 8, WIDTHS[ch])
        core(ch).start()

    def stage_h(ch):
        cp_w[ch].wait()
        part = lax.dot_general(
            recv[ch][...].reshape(NY * CAP, WIDTHS[ch]), wv[ch][...],
            (((1,), (1,)), ((), ())), preferred_element_type=F32,
        )
        if ch == 0:
            acc[...] = part
        elif ch < NCH - 1:
            acc[...] += part
        else:
            back[...] = (acc[...] + part).astype(BF16).reshape(NY, CAP, FF)
            for d in Y_ORDER:
                ret(d).start()

    for ch in range(NCH):
        stage_d(ch)
        stage_h(ch)
        if ch >= 2:
            stage_x(ch - 2)
        stage_core(ch)
    stage_x(NCH - 2)
    stage_x(NCH - 1)
    got[y] = back[y]

    for d in Y_ORDER:
        ret(d).wait_recv()
    cp_got = pltpu.make_async_copy(got, got_hbm, out_sem.at[1])
    cp_got.start()
    for ch in range(NCH):
        for d in Y_ORDER:
            disp(ch, d).wait_send()
        core(ch).wait_send()
        for d in X_ORDER:
            xcopy(ch, d).wait_send()
    for d in Y_ORDER:
        ret(d).wait_send()
    for g in range(NZG):
        for d in Z_ORDER:
            zcopy(g, d).wait_send()
    for g in range(NZG):
        stage_z(g)
    cp_wg = pltpu.make_async_copy(wgo, wg_hbm, out_sem.at[2])
    cp_wg.start()
    cp_pick.wait()
    cp_got.wait()
    cp_wg.wait()


def unpack(got_ref, pick_ref, sum_ref, dh_ref, wg_ref):
    rows = got_ref[...]
    for k in range(pick_ref.shape[0]):
        dh_ref[k] = jnp.dot(pick_ref[k], rows, preferred_element_type=F32).astype(BF16)
    wg_ref[...] = sum_ref[...]


def on_device(out_grad, routes, gates, saved_hidden, down_weight):
    scale = 1.0 / math.sqrt(TOK * NY * NX * NZ * NC * TOP / EXPERTS_ALL)
    any_ = pl.BlockSpec(memory_space=pl.ANY)
    hbm = pl.BlockSpec(memory_space=pltpu.HBM)
    dma = pltpu.SemaphoreType.DMA
    got, pick, wg = pl.pallas_call(
        functools.partial(kernel, scale),
        out_shape=(
            jax.ShapeDtypeStruct((NY, CAP, FF), BF16),
            jax.ShapeDtypeStruct((TOP, TOK, NY * CAP), BF16),
            jax.ShapeDtypeStruct((8, D), F32),
        ),
        in_specs=[hbm] * 5,
        out_specs=(any_, any_, any_),
        scratch_shapes=[
            pltpu.VMEM((TOP, TOK), jnp.int32),
            pltpu.VMEM((TOP, TOK), F32),
            pltpu.VMEM((TOK, D), BF16),
            pltpu.VMEM((NY * CAP, FF), BF16),
            pltpu.VMEM((FF, NY * CAP), BF16),
            [pltpu.VMEM((FF, w), BF16) for w in WIDTHS],
            [pltpu.VMEM((NY, CAP, w), BF16) for w in WIDTHS],
            [pltpu.VMEM((NY, CAP, w), BF16) for w in WIDTHS],
            pltpu.VMEM((NY * CAP, FF), F32),
            pltpu.VMEM((NY, CAP, FF), BF16),
            pltpu.VMEM((NY, CAP, FF), BF16),
            pltpu.VMEM((TOP, TOK, NY * CAP), BF16),
            [pltpu.VMEM((NX * NZ, NC, 8, w), F32) for w in WIDTHS],
            [pltpu.VMEM((NX * NZ, 8, w), F32) for w in WIDTHS],
            [pltpu.VMEM((NX, NZ, w // 16, 128), F32) for w in WIDTHS],
            [pltpu.VMEM((NX, NZ * w // 16, 128), BF16) for w in WIDTHS],
            [pltpu.VMEM((NX - 1, NZ * w // 16, 128), BF16) for w in WIDTHS],
            [pltpu.VMEM((NZ, r, 128), F32) for r in ZROWS],
            [pltpu.VMEM((NZ, r, 128), BF16) for r in ZROWS],
            [pltpu.VMEM((NZ - 1, r, 128), BF16) for r in ZROWS],
            pltpu.VMEM((8, D), F32),
            pltpu.SemaphoreType.REGULAR,
            dma((4,)),
            dma((NCH,)),
            dma((3,)),
            dma((NCH, NY - 1)),
            dma((NCH, NY - 1)),
            dma((NY - 1,)),
            dma((NY - 1,)),
            dma((NCH,)),
            dma((NCH,)),
            dma((NCH, NX - 1)),
            dma((NCH, NX - 1)),
            dma((NZG, NZ - 1)),
            dma((NZG, NZ - 1)),
        ],
        compiler_params=pltpu.CompilerParams(
            collective_id=0, has_side_effects=True, vmem_limit_bytes=VLIM
        ),
        name="moe_down_bwd",
    )(
        out_grad,
        routes.T,
        gates.T,
        saved_hidden.reshape(NY * CAP, FF),
        down_weight[0],
    )
    kb = TOP // UGRID
    dh, wg = pl.pallas_call(
        unpack,
        grid=(UGRID,),
        out_shape=(
            jax.ShapeDtypeStruct((TOP, TOK, FF), BF16),
            jax.ShapeDtypeStruct((8, D), F32),
        ),
        in_specs=[
            pl.BlockSpec((NY * CAP, FF), lambda k: (0, 0)),
            pl.BlockSpec((kb, TOK, NY * CAP), lambda k: (k, 0, 0)),
            pl.BlockSpec((8, D), lambda k: (0, 0)),
        ],
        out_specs=(
            pl.BlockSpec((kb, TOK, FF), lambda k: (k, 0, 0)),
            pl.BlockSpec((8, D), lambda k: (0, 0)),
        ),
        compiler_params=pltpu.CompilerParams(vmem_limit_bytes=VLIM),
        name="unpack",
    )(got.reshape(NY * CAP, FF), pick, wg)
    return dh.transpose(1, 0, 2), wg[None]


def solution(mesh):
    return jax.shard_map(
        on_device,
        mesh=mesh,
        in_specs=(
            P(("expert", "dp"), None),
            P(("expert", "dp"), None),
            P(("expert", "dp"), None),
            P("expert", "dp", None, None, None),
            P("expert", None, None),
        ),
        out_specs=(P(("expert", "dp"), None, None), P("expert", "dp", None)),
        check_vma=False,
    )
```

```python
import functools
import math

import jax
import jax.numpy as jnp
from jax import lax
from jax.experimental import pallas as pl
from jax.experimental.pallas import tpu as pltpu
from jax.sharding import PartitionSpec as P

EXPERTS_ALL = 64
MESH = pl.DeviceIdType.MESH
NY, NX, NZ, NC = 8, 4, 12, 2
CAP = 32
TOK = 128
TOP = 6
D = 2048
FF = 768
WIDTHS = (256,) * 8
ZGROUPS = ((0, 1), (2, 3), (4, 5), (6,), (7,))
NCH = len(WIDTHS)
OFFS = tuple(sum(WIDTHS[:i]) for i in range(NCH))
NZG = len(ZGROUPS)
ZROWS = tuple(sum(WIDTHS[ch] // 16 for ch in g) for g in ZGROUPS)
UGRID = 1
VLIM = 62 << 20
Y_ORDER = (4, 3, 5, 2, 6, 1, 7)
X_ORDER = (2, 1, 3)
Z_ORDER = (6, 5, 7, 4, 8, 3, 9, 2, 10, 1, 11)
F32, BF16 = jnp.float32, jnp.bfloat16


def kernel(
    scale,
    og_hbm, rt_hbm, gt_hbm, hid_hbm, w_hbm,
    got_hbm, pick_hbm, wg_hbm,
    rt_ref, gt_ref, og, hid, hid_t, wv, outb, recv, acc, back, got, pick,
    wg, cr, xf, xs, xr, zf, zs, zr, wgo,
    late_sem, in_sem, w_sem, out_sem,
    ys_sem, yr_sem, bs_sem, br_sem, cs_sem, cr_sem, xs_sem, xr_sem, zs_sem, zr_sem,
):
    y = lax.axis_index("expert")
    dp = lax.axis_index("dp")
    c = lax.rem(dp, NC)
    z = lax.rem(dp // NC, NZ)
    x = dp // (NC * NZ)

    def dev_y(d):
        return (lax.rem(y + d, NY), dp)

    def dev_c():
        return (y, dp + 1 - 2 * c)

    def dev_x(d):
        return (y, (lax.rem(x + d, NX) * NZ + z) * NC + c)

    def dev_z(d):
        return (y, (x * NZ + lax.rem(z + d, NZ)) * NC + c)

    def remote(src, dst, ssem, rsem, dev):
        return pltpu.make_async_remote_copy(
            src_ref=src, dst_ref=dst, send_sem=ssem, recv_sem=rsem,
            device_id=dev, device_id_type=MESH,
        )

    def disp(ch, d):
        return remote(
            outb[ch].at[lax.rem(y + d, NY)], recv[ch].at[y],
            ys_sem.at[ch, d - 1], yr_sem.at[ch, d - 1], dev_y(d),
        )

    def ret(d):
        return remote(
            back.at[lax.rem(y + d, NY)], got.at[y], bs_sem.at[d - 1], br_sem.at[d - 1], dev_y(d)
        )

    def core(ch):
        return remote(wg[ch].at[:, 1 - c], cr[ch], cs_sem.at[ch], cr_sem.at[ch], dev_c())

    def xcopy(ch, d):
        return remote(
            xs[ch].at[lax.rem(x + d, NX)], xr[ch].at[d - 1],
            xs_sem.at[ch, d - 1], xr_sem.at[ch, d - 1], dev_x(d),
        )

    def zcopy(g, d):
        return remote(
            zs[g].at[lax.rem(z + d, NZ)], zr[g].at[d - 1],
            zs_sem.at[g, d - 1], zr_sem.at[g, d - 1], dev_z(d),
        )

    cp_rt = pltpu.make_async_copy(rt_hbm, rt_ref, in_sem.at[2])
    cp_rt.start()
    cp_gt = pltpu.make_async_copy(gt_hbm, gt_ref, in_sem.at[3])
    cp_gt.start()
    cp_og = pltpu.make_async_copy(og_hbm, og, in_sem.at[0])
    cp_og.start()
    barrier = pltpu.get_barrier_semaphore()
    peers = [dev_y(d) for d in Y_ORDER] + [dev_x(d) for d in X_ORDER] + [dev_c()]
    for p in peers:
        pl.semaphore_signal(barrier, inc=1, device_id=p, device_id_type=MESH)
    for d in range(1, NZ):

        @pl.when(z + d < NZ)
        def _(d=d):
            pl.semaphore_signal(barrier, inc=1, device_id=dev_z(d), device_id_type=MESH)

    cp_hid = pltpu.make_async_copy(hid_hbm, hid, in_sem.at[1])
    cp_hid.start()
    cp_w = []
    for ch in range(NCH):
        cp = pltpu.make_async_copy(w_hbm.at[:, pl.ds(OFFS[ch], WIDTHS[ch])], wv[ch], w_sem.at[ch])
        cp.start()
        cp_w.append(cp)

    cp_rt.wait()
    cp_gt.wait()
    routes = rt_ref[...]
    gates = gt_ref[...]
    eid = lax.broadcasted_iota(jnp.int32, (NY, TOK), 0)
    mask = jnp.zeros((NY, TOK), F32)
    gate_e = jnp.zeros((NY, TOK), F32)
    for k in range(TOP):
        hit = routes[k : k + 1, :] == eid
        mask = mask + jnp.where(hit, 1.0, 0.0)
        gate_e = gate_e + jnp.where(hit, gates[k : k + 1, :], 0.0)
    t_row = lax.broadcasted_iota(jnp.int32, (TOK, TOK), 0)
    t_col = lax.broadcasted_iota(jnp.int32, (TOK, TOK), 1)
    before = jnp.where(t_row < t_col, 1.0, 0.0).astype(BF16)
    pos = jnp.dot(mask.astype(BF16), before, preferred_element_type=F32)
    slot = jnp.where(mask > 0.0, pos, -1.0).astype(jnp.int32)
    cid = lax.broadcasted_iota(jnp.int32, (NY, CAP, TOK), 1)
    sel = jnp.where(slot[:, None, :] == cid, 1.0, 0.0)
    gate_row = jnp.sum(sel * gate_e[:, None, :], axis=-1, keepdims=True).reshape(NY * CAP, 1)
    sel = sel.reshape(NY * CAP, TOK).astype(BF16)

    cp_og.wait()
    for ch in range(NCH):
        w = WIDTHS[ch]
        rows = jnp.dot(sel, og[:, OFFS[ch] : OFFS[ch] + w], preferred_element_type=F32)
        outb[ch][...] = (rows * gate_row).astype(BF16).reshape(NY, CAP, w)
        if ch == 0:
            pl.semaphore_wait(barrier, len(peers) + z)
            for d in range(1, NZ):

                @pl.when(z >= d)
                def _(d=d):
                    pl.semaphore_signal(late_sem, inc=1, device_id=dev_z(NZ - d), device_id_type=MESH)

        for d in Y_ORDER:
            disp(ch, d).start()

    for ch in range(NCH):
        recv[ch][y] = outb[ch][y]
    rid = lax.broadcasted_iota(jnp.int32, (NY * CAP, TOK), 0)
    for k in range(TOP):
        hit = routes[k : k + 1, :] == eid
        pos_k = jnp.sum(jnp.where(hit, pos, 0.0), axis=0, keepdims=True).astype(jnp.int32)
        r_k = routes[k : k + 1, :]
        target = jnp.where(r_k < NY, r_k * CAP + pos_k, -1)
        pick[k] = jnp.where(rid == target, 1.0, 0.0).T.astype(BF16)
    cp_hid.wait()
    cp_pick = pltpu.make_async_copy(pick, pick_hbm, out_sem.at[0])
    cp_pick.start()
    hid_t[...] = hid[...].T

    def stage_core(ch):
        w = WIDTHS[ch]
        core(ch).wait_recv()
        s = wg[ch][:, c] + cr[ch][...]
        s = jnp.concatenate([s[:, :, i : i + 128] for i in range(0, w, 128)], axis=1)
        xf[ch][...] = s.reshape(NX, NZ, w // 16, 128)
        xs[ch][...] = s.reshape(NX, NZ * w // 16, 128).astype(BF16)
        for d in X_ORDER:
            xcopy(ch, d).start()

    def stage_x(ch):
        w = WIDTHS[ch]
        for d in X_ORDER:
            xcopy(ch, d).wait_recv()
        s = xf[ch][x].reshape(NZ * w // 16, 128)
        for d in X_ORDER:
            s = s + xr[ch][d - 1].astype(F32)
        s = s.reshape(NZ, w // 16, 128)
        g = next(i for i in range(NZG) if ch in ZGROUPS[i])
        o = sum(WIDTHS[i] // 16 for i in ZGROUPS[g] if i < ch)
        zf[g][:, o : o + w // 16] = s
        if ch == ZGROUPS[g][-1]:
            zs[g][...] = zf[g][...].astype(BF16)
            if g == 0:

                @pl.when(z < NZ - 1)
                def _():
                    pl.semaphore_wait(late_sem, NZ - 1 - z)

            for d in Z_ORDER:
                zcopy(g, d).start()

    def stage_z(g):
        for d in Z_ORDER:
            zcopy(g, d).wait_recv()
        s = zf[g][z]
        for d in Z_ORDER:
            s = s + zr[g][d - 1].astype(F32)
        s = s * scale
        r = 0
        for ch in ZGROUPS[g]:
            for o in range(OFFS[ch], OFFS[ch] + WIDTHS[ch], 128):
                wgo[:, o : o + 128] = s[r : r + 8]
                r += 8

    def stage_d(ch):
        for d in Y_ORDER:
            disp(ch, d).wait_recv()
        rows = recv[ch][...].reshape(NY * CAP, WIDTHS[ch])
        term = jnp.dot(hid_t[...], rows, preferred_element_type=F32)
        wg[ch][...] = term.reshape(NX * NZ, NC, 8, WIDTHS[ch])
        core(ch).start()

    def stage_h(ch):
        cp_w[ch].wait()
        part = lax.dot_general(
            recv[ch][...].reshape(NY * CAP, WIDTHS[ch]), wv[ch][...],
            (((1,), (1,)), ((), ())), preferred_element_type=F32,
        )
        if ch == 0:
            acc[...] = part
        elif ch < NCH - 1:
            acc[...] += part
        else:
            back[...] = (acc[...] + part).astype(BF16).reshape(NY, CAP, FF)
            for d in Y_ORDER:
                ret(d).start()

    for ch in range(NCH):
        stage_d(ch)
        stage_h(ch)
        if ch >= 2:
            stage_x(ch - 2)
        stage_core(ch)
    stage_x(NCH - 2)
    stage_x(NCH - 1)
    got[y] = back[y]

    for d in Y_ORDER:
        ret(d).wait_recv()
    cp_got = pltpu.make_async_copy(got, got_hbm, out_sem.at[1])
    cp_got.start()
    for ch in range(NCH):
        for d in Y_ORDER:
            disp(ch, d).wait_send()
        core(ch).wait_send()
        for d in X_ORDER:
            xcopy(ch, d).wait_send()
    for d in Y_ORDER:
        ret(d).wait_send()
    for g in range(NZG):
        for d in Z_ORDER:
            zcopy(g, d).wait_send()
    for g in range(NZG):
        stage_z(g)
    cp_wg = pltpu.make_async_copy(wgo, wg_hbm, out_sem.at[2])
    cp_wg.start()
    cp_pick.wait()
    cp_got.wait()
    cp_wg.wait()


def unpack(got_ref, pick_ref, sum_ref, dh_ref, wg_ref):
    rows = got_ref[...]
    for k in range(pick_ref.shape[0]):
        dh_ref[k] = jnp.dot(pick_ref[k], rows, preferred_element_type=F32).astype(BF16)
    wg_ref[...] = sum_ref[...]


def on_device(out_grad, routes, gates, saved_hidden, down_weight):
    scale = 1.0 / math.sqrt(TOK * NY * NX * NZ * NC * TOP / EXPERTS_ALL)
    any_ = pl.BlockSpec(memory_space=pl.ANY)
    hbm = pl.BlockSpec(memory_space=pltpu.HBM)
    dma = pltpu.SemaphoreType.DMA
    got, pick, wg = pl.pallas_call(
        functools.partial(kernel, scale),
        out_shape=(
            jax.ShapeDtypeStruct((NY, CAP, FF), BF16),
            jax.ShapeDtypeStruct((TOP, TOK, NY * CAP), BF16),
            jax.ShapeDtypeStruct((8, D), F32),
        ),
        in_specs=[hbm] * 5,
        out_specs=(any_, any_, any_),
        scratch_shapes=[
            pltpu.VMEM((TOP, TOK), jnp.int32),
            pltpu.VMEM((TOP, TOK), F32),
            pltpu.VMEM((TOK, D), BF16),
            pltpu.VMEM((NY * CAP, FF), BF16),
            pltpu.VMEM((FF, NY * CAP), BF16),
            [pltpu.VMEM((FF, w), BF16) for w in WIDTHS],
            [pltpu.VMEM((NY, CAP, w), BF16) for w in WIDTHS],
            [pltpu.VMEM((NY, CAP, w), BF16) for w in WIDTHS],
            pltpu.VMEM((NY * CAP, FF), F32),
            pltpu.VMEM((NY, CAP, FF), BF16),
            pltpu.VMEM((NY, CAP, FF), BF16),
            pltpu.VMEM((TOP, TOK, NY * CAP), BF16),
            [pltpu.VMEM((NX * NZ, NC, 8, w), F32) for w in WIDTHS],
            [pltpu.VMEM((NX * NZ, 8, w), F32) for w in WIDTHS],
            [pltpu.VMEM((NX, NZ, w // 16, 128), F32) for w in WIDTHS],
            [pltpu.VMEM((NX, NZ * w // 16, 128), BF16) for w in WIDTHS],
            [pltpu.VMEM((NX - 1, NZ * w // 16, 128), BF16) for w in WIDTHS],
            [pltpu.VMEM((NZ, r, 128), F32) for r in ZROWS],
            [pltpu.VMEM((NZ, r, 128), BF16) for r in ZROWS],
            [pltpu.VMEM((NZ - 1, r, 128), BF16) for r in ZROWS],
            pltpu.VMEM((8, D), F32),
            pltpu.SemaphoreType.REGULAR,
            dma((4,)),
            dma((NCH,)),
            dma((3,)),
            dma((NCH, NY - 1)),
            dma((NCH, NY - 1)),
            dma((NY - 1,)),
            dma((NY - 1,)),
            dma((NCH,)),
            dma((NCH,)),
            dma((NCH, NX - 1)),
            dma((NCH, NX - 1)),
            dma((NZG, NZ - 1)),
            dma((NZG, NZ - 1)),
        ],
        compiler_params=pltpu.CompilerParams(
            collective_id=0, has_side_effects=True, vmem_limit_bytes=VLIM
        ),
        name="moe_down_bwd",
    )(
        out_grad,
        routes.T,
        gates.T,
        saved_hidden.reshape(NY * CAP, FF),
        down_weight[0],
    )
    kb = TOP // UGRID
    dh, wg = pl.pallas_call(
        unpack,
        grid=(UGRID,),
        out_shape=(
            jax.ShapeDtypeStruct((TOP, TOK, FF), BF16),
            jax.ShapeDtypeStruct((8, D), F32),
        ),
        in_specs=[
            pl.BlockSpec((NY * CAP, FF), lambda k: (0, 0)),
            pl.BlockSpec((kb, TOK, NY * CAP), lambda k: (k, 0, 0)),
            pl.BlockSpec((8, D), lambda k: (0, 0)),
        ],
        out_specs=(
            pl.BlockSpec((kb, TOK, FF), lambda k: (k, 0, 0)),
            pl.BlockSpec((8, D), lambda k: (0, 0)),
        ),
        compiler_params=pltpu.CompilerParams(vmem_limit_bytes=VLIM),
        name="unpack",
    )(got.reshape(NY * CAP, FF), pick, wg)
    return dh.transpose(1, 0, 2), wg[None]


def solution(mesh):
    return jax.shard_map(
        on_device,
        mesh=mesh,
        in_specs=(
            P(("expert", "dp"), None),
            P(("expert", "dp"), None),
            P(("expert", "dp"), None),
            P("expert", "dp", None, None, None),
            P("expert", None, None),
        ),
        out_specs=(P(("expert", "dp"), None, None), P("expert", "dp", None)),
        check_vma=False,
    )
```
